1024 devices in a mesh: seq: 128 (over z, x_lo, core), head: 8 (over x_hi, y).
Axes of the slice: x: 4 (x_hi: 2, x_lo: 2; x = x_hi * 2 + x_lo), y: 4, z: 32, core: 2. Of those that a mesh axis runs over, the one named last changes fastest.
Arguments:
- queries: bfloat16 [131072, 1024], P('seq', 'head'), may hold values from -16 to 16
- keys: bfloat16 [131072, 128], P(('seq', 'head')), may hold values from -4 to 4
- values: bfloat16 [131072, 128], P(('seq', 'head')), may hold values from -6 to 6
- doc_start: int32 [131072], P('seq'), may hold values from 0 to 131071, as said below
Outputs:
- attn_out: bfloat16 [131072, 1024], P('seq', 'head')
- lse: float32 [8, 131072], P('head', 'seq')
The draws below stay inside these ranges and needn't reach their ends.
Inputs may be any that keep to these rules, and one draw needn't show every extreme that they name: doc_start[0] is 0, and for p >= 1 doc_start[p] is either p or doc_start[p - 1]; the first document covers at least the first 3072 tokens; the last token always begins a document of its own.
All inputs are finite; a program needn't handle non-finite values.
Results may differ from the reference program's by a relative error of at most 0.0045.
Values may be sent and summed in bfloat16 or wider, within the bound.
No kernel may reach another device: no remote copies, remote signals or barrier semaphores. Data moves between devices by JAX's collectives and lax.ppermute only.
A program may use at most 32 MiB of HBM per device.

```python
import math
import jax
import jax.numpy as jnp
from jax import lax

HQ = 8
HD = 128
C = 1024
S = 131072
N_SEQ = 128


def starts_mask(key):
    bits = jax.random.randint(jax.random.fold_in(key, 101), (S,), 0, 2 * C)
    places = jnp.arange(S)
    return (bits == 0) & (places >= 3 * C) | (places == 0) | (places == S - 1)


def draw_doc_start(key, part):
    starts = starts_mask(key)
    marked = jnp.where(starts, jnp.arange(S, dtype=jnp.int32), 0)
    return lax.cummax(marked, axis=0).astype(jnp.int32)


def draw_keys(key, part):
    inner = jax.random.fold_in(key, 12)
    base = jnp.clip(jax.random.normal(inner, (S, HD), jnp.float32), -4.0, 4.0)
    return base.astype(jnp.bfloat16)


def draw_queries(key, part):
    inner = jax.random.fold_in(key, 11)
    base = jnp.clip(jax.random.normal(inner, (S, HQ, HD), jnp.float32), -4.0, 4.0)
    return base.reshape(S, HQ * HD).astype(jnp.bfloat16)


def level_of(rng, extent, pieces, low, top_value):
    level = 1.0
    for axis_at, shards_of in pieces:
        steps = jax.random.uniform(jax.random.fold_in(jax.random.fold_in(rng, 6), axis_at), (shards_of,), jnp.float32, low / len(pieces), top_value / len(pieces))
        level = level * jnp.repeat(jnp.exp(steps), extent[axis_at] // shards_of).reshape((-1,) + (1,) * (len(extent) - 1 - axis_at))
    return level


def bell_draw(key, shape, scale, bound, shards=(), held_as=jnp.bfloat16):
    drawn = jax.random.normal(key, shape, jnp.float32) * scale
    if len(shards) > 0:
        drawn = level_of(key, shape, shards, -0.22, 0.18) * drawn
    return jnp.clip(drawn, min=-bound, max=bound).astype(held_as)


def setup_inputs(seed: int = 0) -> dict:
    arg_keys = jax.random.split(jax.random.key(seed), 5)
    queries = draw_queries(jax.random.fold_in(arg_keys[4], 71), 0)
    keys = draw_keys(jax.random.fold_in(arg_keys[4], 71), 0)
    values = bell_draw(arg_keys[2], (S, HD), 1.0, 6.0, ((0, 1024),))
    doc_start = draw_doc_start(jax.random.fold_in(arg_keys[4], 71), 0)
    return {"queries": queries, "keys": keys, "values": values, "doc_start": doc_start}


negative_fill = -1e+30

def reference(queries, keys, values, doc_start):
    score_scale = 1.0 / math.sqrt(HD)
    key_padded = jnp.concatenate([jnp.zeros((2 * C, HD), keys.dtype), keys], axis=0)
    value_padded = jnp.concatenate([jnp.zeros((2 * C, HD), values.dtype), values], axis=0)

    def per_span(index):
        first = (index * C).astype(jnp.int32)
        query_rows = lax.dynamic_slice_in_dim(queries, first, C, 0).reshape(C, HQ, HD).astype(jnp.float32)
        key_rows = lax.dynamic_slice_in_dim(key_padded, first, 3 * C, 0).astype(jnp.float32)
        value_rows = lax.dynamic_slice_in_dim(value_padded, first, 3 * C, 0).astype(jnp.float32)
        start_rows = lax.dynamic_slice_in_dim(doc_start, first, C, 0)
        query_pos = first + jnp.arange(C, dtype=jnp.int32)
        key_pos = first - 2 * C + jnp.arange(3 * C, dtype=jnp.int32)
        visible = (key_pos[None, :] <= query_pos[:, None]) & (key_pos[None, :] >= start_rows[:, None])
        scores = jnp.einsum('qhd,kd->hqk', query_rows, key_rows) * score_scale
        scores = jnp.where(visible[None], scores, negative_fill)
        row_max = lax.optimization_barrier(jnp.max(scores, axis=-1))
        weights = jnp.where(visible[None], jnp.exp(scores - row_max[..., None]), 0.0)
        total = lax.optimization_barrier(jnp.sum(weights, axis=-1))
        rounded = weights.astype(jnp.bfloat16).astype(jnp.float32)
        mixed = jnp.einsum('hqk,kd->hqd', rounded, value_rows) / total[..., None]
        normed = mixed.transpose(1, 0, 2).reshape(C, HQ * HD).astype(jnp.bfloat16)
        return (normed, row_max + jnp.log(total))
    normed, log_total = lax.map(per_span, jnp.arange(N_SEQ, dtype=jnp.int32))
    return (normed.reshape(S, HQ * HD), log_total.transpose(1, 0, 2).reshape(HQ, S))
```

```python
import functools
import math

import jax
import jax.numpy as jnp
from jax import lax
from jax.experimental import pallas as pl
from jax.experimental.pallas import tpu as pltpu
from jax.sharding import PartitionSpec as P

negative_fill = -1e30
ROWS = 256


def dot_nt(a, b):
    return lax.dot_general(a, b, (((1,), (1,)), ((), ())), preferred_element_type=jnp.float32)


def attend_kernel(place_ref, q_ref, start_ref, gathered_ref, out_ref, lse_ref, vals_ref, starts_ref):
    span, head_dim = q_ref.shape
    shard = gathered_ref.shape[3] // 2
    pos, core = place_ref[0], place_ref[1]
    scale = 1.0 / math.sqrt(head_dim)
    to_log2 = scale * math.log2(math.e)
    where = ((core, 0), (1 - core, 1 - core), (core, 1))
    for i, (c, j) in enumerate(where):
        vals_ref[i, :, :head_dim] = gathered_ref[c, :, j, shard:, :].reshape(span, head_dim)
    vals_ref[:, :, head_dim:] = jnp.ones((3, span, head_dim), vals_ref.dtype)
    starts_ref[...] = jnp.broadcast_to(start_ref[...], (head_dim, span)).T
    keys = [gathered_ref[c, :, j, :shard, :].reshape(span, head_dim) for c, j in where]

    for r in range(span // ROWS):
        rows = slice(r * ROWS, (r + 1) * ROWS)
        q = q_ref[rows, :]
        starts = starts_ref[rows, :1]
        query_pos = pos * span + r * ROWS + lax.broadcasted_iota(jnp.int32, (ROWS, 1), 0)
        parts = []
        for i in range(3):
            width = (r + 1) * ROWS if i == 0 else span
            scores = dot_nt(q, keys[i][:width])
            key_pos = (pos - i) * span + lax.broadcasted_iota(jnp.int32, (ROWS, width), 1)
            visible = key_pos >= starts
            if i == 0:
                visible &= key_pos <= query_pos
            parts.append(jnp.where(visible, scores, negative_fill))
        top = functools.reduce(jnp.maximum, [jnp.max(s, axis=1, keepdims=True) for s in parts])
        total = 0.0
        for i, s in enumerate(parts):
            weights = jnp.exp2((s - top) * to_log2).astype(jnp.bfloat16)
            total += jnp.dot(weights, vals_ref[i, : s.shape[1]], preferred_element_type=jnp.float32)
        sums = total[:, head_dim:]
        out_ref[rows, :] = (total[:, :head_dim] / sums).astype(out_ref.dtype)
        lse_ref[:, rows] = (top * scale + jnp.log(sums)).T[:1]


def attend(place, queries, doc_start, gathered):
    span, head_dim = queries.shape
    vmem = pl.BlockSpec(memory_space=pltpu.VMEM)
    return pl.pallas_call(
        attend_kernel,
        out_shape=(
            jax.ShapeDtypeStruct((span, head_dim), jnp.bfloat16),
            jax.ShapeDtypeStruct((1, span), jnp.float32),
        ),
        in_specs=[pl.BlockSpec(memory_space=pltpu.SMEM), vmem, vmem, vmem],
        out_specs=(vmem, vmem),
        scratch_shapes=[
            pltpu.VMEM((3, span, 2 * head_dim), jnp.bfloat16),
            pltpu.VMEM((span, head_dim), jnp.int32),
        ],
        compiler_params=pltpu.CompilerParams(vmem_limit_bytes=32 * 1024 * 1024),
    )(place, queries, doc_start, gathered)


def body(queries, keys, values, doc_start):
    span = doc_start.shape[0]
    pos = lax.axis_index("seq")
    count, heads = lax.axis_size("seq"), lax.axis_size("head")
    own = jnp.concatenate([keys, values], axis=0)
    shifted = lax.ppermute(own, "seq", [(i, i + 2) for i in range(count - 2)])
    pair = jnp.stack([own, shifted])
    block = lax.all_to_all(jnp.broadcast_to(pair[None], (heads,) + pair.shape), "head", 0, 0)
    gathered = lax.all_gather(
        block, "seq", axis=0, axis_index_groups=[[i, i + 1] for i in range(0, count, 2)]
    )
    place = jnp.stack([pos, pos % 2]).astype(jnp.int32)
    return attend(place, queries, doc_start.reshape(1, span), gathered)


def solution(mesh):
    in_specs = (P("seq", "head"), P(("seq", "head"), None), P(("seq", "head"), None), P("seq"))
    out_specs = (P("seq", "head"), P("head", "seq"))
    return jax.shard_map(body, mesh=mesh, in_specs=in_specs, out_specs=out_specs, check_vma=False)
```

```python
import math

import jax
import jax.numpy as jnp
from jax import lax
from jax.experimental import pallas as pl
from jax.experimental.pallas import tpu as pltpu
from jax.sharding import PartitionSpec as P

negative_fill = -1e30
ROWS = 256
VMEM = pl.BlockSpec(memory_space=pltpu.VMEM)
SMEM = pl.BlockSpec(memory_space=pltpu.SMEM)
LN2 = math.log(2.0)


def dot_nt(a, b):
    return lax.dot_general(a, b, (((1,), (1,)), ((), ())), preferred_element_type=jnp.float32)


def scores_of(q, keys, key_base, starts, query_pos):
    rows, width = q.shape[0], keys.shape[0]
    to_log2 = math.log2(math.e) / math.sqrt(q.shape[1])
    key_pos = key_base + lax.broadcasted_iota(jnp.int32, (rows, width), 1)
    visible = key_pos >= starts
    if query_pos is not None:
        visible &= key_pos <= query_pos
    return jnp.where(visible, dot_nt(q, keys) * to_log2, negative_fill)


def weigh(scores, values, top):
    weights = jnp.exp2(scores - top)
    total = jnp.sum(weights, axis=1, keepdims=True)
    mixed = jnp.dot(weights.astype(jnp.bfloat16), values, preferred_element_type=jnp.float32)
    return total, mixed


def block_of(ref, which, kind):
    shards, _, _, shard, head_dim = ref.shape
    return ref[:, which, kind].reshape(shards * shard, head_dim)


def first_kernel(pos_ref, q_ref, start_ref, pair_ref, mixed_ref, log_ref, starts_ref):
    span, head_dim = q_ref.shape
    pos = pos_ref[0]
    starts_ref[...] = jnp.broadcast_to(start_ref[...], (head_dim, span)).T
    own_keys, own_values = block_of(pair_ref, 0, 0), block_of(pair_ref, 0, 1)
    far_keys, far_values = block_of(pair_ref, 1, 0), block_of(pair_ref, 1, 1)
    for r in range(span // ROWS):
        rows, width = slice(r * ROWS, (r + 1) * ROWS), (r + 1) * ROWS
        q, starts = q_ref[rows, :], starts_ref[rows, :1]
        query_pos = pos * span + r * ROWS + lax.broadcasted_iota(jnp.int32, (ROWS, 1), 0)
        own = scores_of(q, own_keys[:width], pos * span, starts, query_pos)
        far = scores_of(q, far_keys, (pos - 2) * span, starts, None)
        top = jnp.maximum(
            jnp.max(own, axis=1, keepdims=True), jnp.max(far, axis=1, keepdims=True)
        )
        own_total, own_mixed = weigh(own, own_values[:width], top)
        far_total, far_mixed = weigh(far, far_values, top)
        total = own_total + far_total
        mixed_ref[rows, :] = (own_mixed + far_mixed) / total
        log_ref[rows, :] = jnp.broadcast_to(top + jnp.log2(total), (ROWS, head_dim))


def second_kernel(pos_ref, q_ref, start_ref, other_ref, mixed_ref, log_ref, out_ref, lse_ref, starts_ref):
    span, head_dim = q_ref.shape
    pos = pos_ref[0]
    which = 1 - lax.rem(pos, 2)
    starts_ref[...] = jnp.broadcast_to(start_ref[...], (head_dim, span)).T
    keys, values = block_of(other_ref, which, 0), block_of(other_ref, which, 1)
    for r in range(span // ROWS):
        rows = slice(r * ROWS, (r + 1) * ROWS)
        scores = scores_of(q_ref[rows, :], keys, (pos - 1) * span, starts_ref[rows, :1], None)
        logs = log_ref[rows, :1]
        top = jnp.maximum(logs, jnp.max(scores, axis=1, keepdims=True))
        before = jnp.exp2(logs - top)
        total, mixed = weigh(scores, values, top)
        total += before
        out_ref[rows, :] = ((mixed_ref[rows, :] * before + mixed) / total).astype(out_ref.dtype)
        lse = (top + jnp.log2(total)) * LN2
        lse_ref[:, rows] = jnp.broadcast_to(lse, (ROWS, head_dim)).T[:1]


def attend_first(pos, queries, starts, pair):
    span, head_dim = queries.shape
    state = jax.ShapeDtypeStruct((span, head_dim), jnp.float32)
    return pl.pallas_call(
        first_kernel,
        out_shape=(state, state),
        in_specs=[SMEM, VMEM, VMEM, VMEM],
        out_specs=(VMEM, VMEM),
        scratch_shapes=[pltpu.VMEM((span, head_dim), jnp.int32)],
        compiler_params=pltpu.CompilerParams(vmem_limit_bytes=32 * 1024 * 1024),
        cost_estimate=pl.CostEstimate(
            flops=4 * span * 2 * span * head_dim, bytes_accessed=3 << 20, transcendentals=2 * span * span
        ),
    )(pos, queries, starts, pair)


def attend_second(pos, queries, starts, other, mixed, logs):
    span, head_dim = queries.shape
    return pl.pallas_call(
        second_kernel,
        out_shape=(
            jax.ShapeDtypeStruct((span, head_dim), jnp.bfloat16),
            jax.ShapeDtypeStruct((1, span), jnp.float32),
        ),
        in_specs=[SMEM, VMEM, VMEM, VMEM, VMEM, VMEM],
        out_specs=(VMEM, VMEM),
        scratch_shapes=[pltpu.VMEM((span, head_dim), jnp.int32)],
        compiler_params=pltpu.CompilerParams(vmem_limit_bytes=32 * 1024 * 1024),
        cost_estimate=pl.CostEstimate(
            flops=4 * span * span * head_dim, bytes_accessed=3 << 20, transcendentals=span * span
        ),
    )(pos, queries, starts, other, mixed, logs)


def stacked(first, second):
    shape = (2,) + first.shape
    at = lax.broadcasted_iota(jnp.int32, shape, 0)
    return jnp.where(at == 0, first[None], second[None])


def body(queries, keys, values, doc_start):
    span = doc_start.shape[0]
    pos = lax.axis_index("seq")
    count, heads = lax.axis_size("seq"), lax.axis_size("head")
    own = stacked(keys, values)
    far = lax.ppermute(own, "seq", [(i, i + 2) for i in range(count - 2)])
    pair = stacked(own, far)
    pair = lax.all_to_all(jnp.broadcast_to(pair[None], (heads,) + pair.shape), "head", 0, 0)
    other = lax.ppermute(pair, "seq", [(i, i ^ 1) for i in range(count)])
    place, starts = jnp.stack([pos]).astype(jnp.int32), doc_start.reshape(1, span)
    mixed, logs = attend_first(place, queries, starts, pair)
    return attend_second(place, queries, starts, other, mixed, logs)


def solution(mesh):
    in_specs = (P("seq", "head"), P(("seq", "head"), None), P(("seq", "head"), None), P("seq"))
    out_specs = (P("seq", "head"), P("head", "seq"))
    return jax.shard_map(body, mesh=mesh, in_specs=in_specs, out_specs=out_specs, check_vma=False)
```

```python
import math

import jax
import jax.numpy as jnp
from jax import lax
from jax.experimental import pallas as pl
from jax.experimental.pallas import tpu as pltpu
from jax.sharding import PartitionSpec as P

negative_fill = -1e30
ROWS = 256
VMEM = pl.BlockSpec(memory_space=pltpu.VMEM)
SMEM = pl.BlockSpec(memory_space=pltpu.SMEM)
HBM = pl.BlockSpec(memory_space=pltpu.HBM)
LN2 = math.log(2.0)
VMEM_LIMIT = 32 * 1024 * 1024
AXES = ("seq", "head")


def dot_nt(a, b):
    return lax.dot_general(a, b, (((1,), (1,)), ((), ())), preferred_element_type=jnp.float32)


def hide(products, key_base, starts, query_pos=None):
    to_log2 = math.log2(math.e) / math.sqrt(128)
    key_pos = key_base + lax.broadcasted_iota(jnp.int32, products.shape, 1)
    visible = key_pos >= starts
    if query_pos is not None:
        visible &= key_pos <= query_pos
    return jnp.where(visible, products * to_log2, negative_fill)


def top_of(scores):
    return jnp.max(scores, axis=1, keepdims=True)


def weigh(scores, values, top):
    weights = jnp.exp2(scores - top)
    total = jnp.sum(weights, axis=1, keepdims=True)
    mixed = jnp.dot(weights.astype(jnp.bfloat16), values, preferred_element_type=jnp.float32)
    return total, mixed


def block_of(ref, side, kind):
    rows = ref.shape[0] * ref.shape[2] * ref.shape[4]
    return ref[:, side, :, kind].reshape(rows, ref.shape[5])


def first_kernel(pos_ref, q_ref, start_ref, held_ref, mixed_ref, log_ref, starts_ref, row_ref, sem):
    span, head_dim = q_ref.shape
    pos = pos_ref[0]
    side = lax.rem(pos // 2, 2)
    fetch = pltpu.make_async_copy(start_ref, row_ref, sem)
    fetch.start()
    own_keys, own_values = block_of(held_ref, side, 0), block_of(held_ref, side, 1)
    far_keys, far_values = block_of(held_ref, 1 - side, 0), block_of(held_ref, 1 - side, 1)

    def products_of(r):
        rows = slice(r * ROWS, (r + 1) * ROWS)
        q = q_ref[rows, :]
        past = dot_nt(q, own_keys[: r * ROWS]) if r else None
        return dot_nt(q, own_keys[rows]), past, dot_nt(q, far_keys)

    upcoming = products_of(0)
    fetch.wait()
    starts_ref[...] = jnp.broadcast_to(row_ref[...], (head_dim, span)).T
    for r in range(span // ROWS):
        rows = slice(r * ROWS, (r + 1) * ROWS)
        near, past, far = upcoming
        if (r + 1) * ROWS < span:
            upcoming = products_of(r + 1)
        starts = starts_ref[rows, :1]
        query_pos = pos * span + r * ROWS + lax.broadcasted_iota(jnp.int32, (ROWS, 1), 0)
        parts = [
            (hide(near, pos * span + r * ROWS, starts, query_pos), own_values[rows]),
            (hide(far, (pos - 2) * span, starts), far_values),
        ]
        if r:
            parts.append((hide(past, pos * span, starts), own_values[: r * ROWS]))
        top = top_of(parts[0][0])
        for scores, _ in parts[1:]:
            top = jnp.maximum(top, top_of(scores))
        total, mixed = 0.0, 0.0
        for scores, values in parts:
            part_total, part_mixed = weigh(scores, values, top)
            total += part_total
            mixed += part_mixed
        mixed_ref[rows, :] = mixed / total
        log_ref[rows, :] = jnp.broadcast_to(top + jnp.log2(total), (ROWS, head_dim))


def second_kernel(pos_ref, q_ref, starts_ref, other_ref, mixed_ref, log_ref, out_ref, lse_ref, out_vmem, lse_vmem, sems):
    span, head_dim = q_ref.shape
    pos = pos_ref[0]
    side, odd = lax.rem(pos // 2, 2), lax.rem(pos, 2)
    side = jnp.where(odd == 1, side, 1 - side)
    keys, values = block_of(other_ref, side, 0), block_of(other_ref, side, 1)
    sends = []
    for r in range(span // ROWS):
        rows = slice(r * ROWS, (r + 1) * ROWS)
        scores = hide(dot_nt(q_ref[rows, :], keys), (pos - 1) * span, starts_ref[rows, :1])
        logs = log_ref[rows, :1]
        top = jnp.maximum(logs, top_of(scores))
        before = jnp.exp2(logs - top)
        total, mixed = weigh(scores, values, top)
        total += before
        out_vmem[rows, :] = ((mixed_ref[rows, :] * before + mixed) / total).astype(out_ref.dtype)
        sends.append(pltpu.make_async_copy(out_vmem.at[rows], out_ref.at[rows], sems.at[r]))
        sends[-1].start()
        lse = (top + jnp.log2(total)) * LN2
        lse_vmem[:, rows] = jnp.broadcast_to(lse, (ROWS, head_dim)).T[:1]
    sends.append(pltpu.make_async_copy(lse_vmem, lse_ref, sems.at[span // ROWS]))
    sends[-1].start()
    for send in sends:
        send.wait()


def attend(pos, queries, doc_start, held, other):
    span, head_dim = queries.shape
    state = jax.ShapeDtypeStruct((span, head_dim), jnp.float32)
    params = pltpu.CompilerParams(vmem_limit_bytes=VMEM_LIMIT)

    def cost(blocks):
        return pl.CostEstimate(
            flops=4 * blocks * span * span * head_dim,
            bytes_accessed=3 << 20,
            transcendentals=blocks * span * span,
        )

    mixed, logs, starts = pl.pallas_call(
        first_kernel,
        out_shape=(state, state, jax.ShapeDtypeStruct((span, head_dim), jnp.int32)),
        in_specs=[SMEM, VMEM, HBM, VMEM],
        out_specs=(VMEM, VMEM, VMEM),
        scratch_shapes=[pltpu.VMEM((1, span), jnp.int32), pltpu.SemaphoreType.DMA],
        compiler_params=params,
        cost_estimate=cost(2),
    )(pos, queries, doc_start.reshape(1, span), held)
    return pl.pallas_call(
        second_kernel,
        out_shape=(
            jax.ShapeDtypeStruct((span, head_dim), jnp.bfloat16),
            jax.ShapeDtypeStruct((1, span), jnp.float32),
        ),
        in_specs=[SMEM, VMEM, VMEM, VMEM, VMEM, VMEM],
        out_specs=(HBM, HBM),
        scratch_shapes=[
            pltpu.VMEM((span, head_dim), jnp.bfloat16),
            pltpu.VMEM((1, span), jnp.float32),
            pltpu.SemaphoreType.DMA((span // ROWS + 1,)),
        ],
        compiler_params=params,
        cost_estimate=cost(1),
    )(pos, queries, starts, other, mixed, logs)


def body(queries, keys, values, doc_start):
    span, (shard, head_dim) = doc_start.shape[0], keys.shape
    count, heads = lax.axis_size("seq"), lax.axis_size("head")
    pos = lax.axis_index("seq")
    width = heads // 2
    own = jnp.where(lax.broadcasted_iota(jnp.int32, (2, shard, head_dim), 0) == 0, keys[None], values[None])
    upward = [(i, i + 4) for i in range(count - 4) if i % 4 >= 2]
    below = lax.ppermute(own, "seq", upward)
    to_side = lax.broadcasted_iota(jnp.int32, (2, 2, width) + own.shape, 1)
    sent = jnp.where((to_side == 0) & (pos % 4 >= 2), below, own)
    slabs = [
        [(z * 4 + side * 2 + core) * heads + high * width + y for high in range(2) for side in range(2) for y in range(width)]
        for z in range(count // 4)
        for core in range(2)
    ]
    held = lax.all_to_all(sent.reshape((4 * width,) + own.shape), AXES, 0, 0, axis_index_groups=slabs)
    held = held.reshape(sent.shape)
    other = lax.ppermute(held, "seq", [(i, i ^ 1) for i in range(count)])
    return attend(jnp.stack([pos]).astype(jnp.int32), queries, doc_start, held, other)


def solution(mesh):
    in_specs = (P("seq", "head"), P(("seq", "head"), None), P(("seq", "head"), None), P("seq"))
    out_specs = (P("seq", "head"), P("head", "seq"))
    return jax.shard_map(body, mesh=mesh, in_specs=in_specs, out_specs=out_specs, check_vma=False)
```

```python
import math

import jax
import jax.numpy as jnp
from jax import lax
from jax.experimental import pallas as pl
from jax.experimental.pallas import tpu as pltpu
from jax.sharding import PartitionSpec as P

negative_fill = -1e30
ROWS = 256
VMEM = pl.BlockSpec(memory_space=pltpu.VMEM)
SMEM = pl.BlockSpec(memory_space=pltpu.SMEM)
HBM = pl.BlockSpec(memory_space=pltpu.HBM)
LN2 = math.log(2.0)
VMEM_LIMIT = 32 * 1024 * 1024
AXES = ("seq", "head")


def dot_nt(a, b):
    return lax.dot_general(a, b, (((1,), (1,)), ((), ())), preferred_element_type=jnp.float32)


def hide(products, key_base, starts, query_pos=None):
    to_log2 = math.log2(math.e) / math.sqrt(128)
    key_pos = key_base + lax.broadcasted_iota(jnp.int32, products.shape, 1)
    visible = key_pos >= starts
    if query_pos is not None:
        visible &= key_pos <= query_pos
    return jnp.where(visible, products * to_log2, negative_fill)


def top_of(scores):
    return jnp.max(scores, axis=1, keepdims=True)


def weigh(scores, values, top):
    weights = jnp.exp2(scores - top).astype(jnp.bfloat16)
    return jnp.dot(weights, values, preferred_element_type=jnp.float32)


def beside_ones(values, both_ref):
    head_dim = values.shape[1]
    both_ref[:, :head_dim] = values
    both_ref[:, head_dim:] = jnp.ones_like(values)


def block_of(ref, side, kind):
    rows = ref.shape[0] * ref.shape[2] * ref.shape[4]
    return ref[:, side, :, kind].reshape(rows, ref.shape[5])


def first_kernel(pos_ref, q_ref, start_ref, held_ref, mixed_ref, log_ref, starts_ref, row_ref, own_ref, far_ref, sem):
    span, head_dim = q_ref.shape
    pos = pos_ref[0]
    side = lax.rem(pos // 2, 2)
    fetch = pltpu.make_async_copy(start_ref, row_ref, sem)
    fetch.start()
    own_keys, far_keys = block_of(held_ref, side, 0), block_of(held_ref, 1 - side, 0)

    def products_of(r):
        rows = slice(r * ROWS, (r + 1) * ROWS)
        q = q_ref[rows, :]
        past = dot_nt(q, own_keys[: r * ROWS]) if r else None
        return dot_nt(q, own_keys[rows]), past, dot_nt(q, far_keys)

    upcoming = products_of(0)
    beside_ones(block_of(held_ref, side, 1), own_ref)
    beside_ones(block_of(held_ref, 1 - side, 1), far_ref)
    fetch.wait()
    starts_ref[...] = jnp.broadcast_to(row_ref[...], (head_dim, span)).T
    for r in range(span // ROWS):
        rows = slice(r * ROWS, (r + 1) * ROWS)
        near, past, far = upcoming
        if (r + 1) * ROWS < span:
            upcoming = products_of(r + 1)
        starts = starts_ref[rows, :1]
        query_pos = pos * span + r * ROWS + lax.broadcasted_iota(jnp.int32, (ROWS, 1), 0)
        parts = [
            (hide(near, pos * span + r * ROWS, starts, query_pos), own_ref[rows, :]),
            (hide(far, (pos - 2) * span, starts), far_ref[...]),
        ]
        if r:
            parts.append((hide(past, pos * span, starts), own_ref[: r * ROWS, :]))
        top = top_of(parts[0][0])
        for scores, _ in parts[1:]:
            top = jnp.maximum(top, top_of(scores))
        sums = sum(weigh(scores, values, top) for scores, values in parts)
        total = sums[:, head_dim:]
        mixed_ref[rows, :] = sums[:, :head_dim] / total
        log_ref[rows, :] = top + jnp.log2(total)


def second_kernel(pos_ref, q_ref, starts_ref, other_ref, mixed_ref, log_ref, out_ref, lse_ref, both_ref, out_vmem, lse_vmem, sems):
    span, head_dim = q_ref.shape
    pos = pos_ref[0]
    side, odd = lax.rem(pos // 2, 2), lax.rem(pos, 2)
    side = jnp.where(odd == 1, side, 1 - side)
    keys = block_of(other_ref, side, 0)
    products = [dot_nt(q_ref[:ROWS, :], keys)]
    beside_ones(block_of(other_ref, side, 1), both_ref)
    sends = []
    for r in range(span // ROWS):
        rows = slice(r * ROWS, (r + 1) * ROWS)
        scores = hide(products.pop(0), (pos - 1) * span, starts_ref[rows, :1])
        if (r + 1) * ROWS < span:
            products.append(dot_nt(q_ref[(r + 1) * ROWS : (r + 2) * ROWS, :], keys))
        top = top_of(scores)
        sums = weigh(scores, both_ref[...], top)
        logs = log_ref[rows, :]
        joint = jnp.maximum(logs, top)
        before, after = jnp.exp2(logs - joint), jnp.exp2(top - joint)
        total = sums[:, head_dim:] * after + before
        mixed = mixed_ref[rows, :] * before + sums[:, :head_dim] * after
        out_vmem[rows, :] = (mixed / total).astype(out_ref.dtype)
        sends.append(pltpu.make_async_copy(out_vmem.at[rows], out_ref.at[rows], sems.at[r]))
        sends[-1].start()
        lse_vmem[:, rows] = row_of((joint + jnp.log2(total)) * LN2)
    sends.append(pltpu.make_async_copy(lse_vmem, lse_ref, sems.at[span // ROWS]))
    sends[-1].start()
    for send in sends:
        send.wait()


def row_of(column):
    rows, lanes = column.shape
    at = lax.broadcasted_iota(jnp.int32, (lanes, lanes), 0) == lax.broadcasted_iota(jnp.int32, (lanes, lanes), 1)
    picked = [
        jnp.sum(jnp.where(at, column[i : i + lanes], 0.0), axis=0, keepdims=True) for i in range(0, rows, lanes)
    ]
    return jnp.concatenate(picked, axis=1)


def attend(pos, queries, doc_start, held, other):
    span, head_dim = queries.shape
    state = jax.ShapeDtypeStruct((span, head_dim), jnp.float32)
    params = pltpu.CompilerParams(vmem_limit_bytes=VMEM_LIMIT)
    both = pltpu.VMEM((span, 2 * head_dim), jnp.bfloat16)

    def cost(blocks):
        return pl.CostEstimate(
            flops=4 * blocks * span * span * head_dim,
            bytes_accessed=3 << 20,
            transcendentals=blocks * span * span,
        )

    mixed, logs, starts = pl.pallas_call(
        first_kernel,
        out_shape=(state, state, jax.ShapeDtypeStruct((span, head_dim), jnp.int32)),
        in_specs=[SMEM, VMEM, HBM, VMEM],
        out_specs=(VMEM, VMEM, VMEM),
        scratch_shapes=[pltpu.VMEM((1, span), jnp.int32), both, both, pltpu.SemaphoreType.DMA],
        compiler_params=params,
        cost_estimate=cost(2),
    )(pos, queries, doc_start.reshape(1, span), held)
    return pl.pallas_call(
        second_kernel,
        out_shape=(
            jax.ShapeDtypeStruct((span, head_dim), jnp.bfloat16),
            jax.ShapeDtypeStruct((1, span), jnp.float32),
        ),
        in_specs=[SMEM, VMEM, VMEM, VMEM, VMEM, VMEM],
        out_specs=(HBM, HBM),
        scratch_shapes=[
            both,
            pltpu.VMEM((span, head_dim), jnp.bfloat16),
            pltpu.VMEM((1, span), jnp.float32),
            pltpu.SemaphoreType.DMA((span // ROWS + 1,)),
        ],
        compiler_params=params,
        cost_estimate=cost(1),
    )(pos, queries, starts, other, mixed, logs)


def body(queries, keys, values, doc_start):
    span, (shard, head_dim) = doc_start.shape[0], keys.shape
    count, heads = lax.axis_size("seq"), lax.axis_size("head")
    pos = lax.axis_index("seq")
    width = heads // 2
    own = jnp.where(lax.broadcasted_iota(jnp.int32, (2, shard, head_dim), 0) == 0, keys[None], values[None])
    upward = [(i, i + 4) for i in range(count - 4) if i % 4 >= 2]
    below = lax.ppermute(own, "seq", upward)
    to_side = lax.broadcasted_iota(jnp.int32, (2, 2, width) + own.shape, 1)
    sent = jnp.where((to_side == 0) & (pos % 4 >= 2), below, own)
    slabs = [
        [(z * 4 + side * 2 + core) * heads + high * width + y for high in range(2) for side in range(2) for y in range(width)]
        for z in range(count // 4)
        for core in range(2)
    ]
    held = lax.all_to_all(sent.reshape((4 * width,) + own.shape), AXES, 0, 0, axis_index_groups=slabs)
    held = held.reshape(sent.shape)
    other = lax.ppermute(held, "seq", [(i, i ^ 1) for i in range(count)])
    return attend(jnp.stack([pos]).astype(jnp.int32), queries, doc_start, held, other)


def solution(mesh):
    in_specs = (P("seq", "head"), P(("seq", "head"), None), P(("seq", "head"), None), P("seq"))
    out_specs = (P("seq", "head"), P("head", "seq"))
    return jax.shard_map(body, mesh=mesh, in_specs=in_specs, out_specs=out_specs, check_vma=False)
```

```python
import math

import jax
import jax.numpy as jnp
from jax import lax
from jax.experimental import pallas as pl
from jax.experimental.pallas import tpu as pltpu
from jax.sharding import PartitionSpec as P

negative_fill = -1e30
ROWS = 256
VMEM = pl.BlockSpec(memory_space=pltpu.VMEM)
SMEM = pl.BlockSpec(memory_space=pltpu.SMEM)
HBM = pl.BlockSpec(memory_space=pltpu.HBM)
LN2 = math.log(2.0)
VMEM_LIMIT = 32 * 1024 * 1024
HEAD_DIM = 128
TO_LOG2 = math.log2(math.e) / math.sqrt(HEAD_DIM)
AXES = ("seq", "head")


def dot_nt(a, b):
    return lax.dot_general(a, b, (((1,), (1,)), ((), ())), preferred_element_type=jnp.float32)


def hide(products, key_base, starts, query_pos=None):
    key_pos = key_base + lax.broadcasted_iota(jnp.int32, products.shape, 1)
    visible = key_pos >= starts
    if query_pos is not None:
        visible &= key_pos <= query_pos
    return jnp.where(visible, products, negative_fill)


def top_of(*parts, lanes=128):
    pieces = [scores[:, i : i + lanes] for scores in parts for i in range(0, scores.shape[1], lanes)]
    while len(pieces) > 1:
        pieces = [jnp.maximum(*pieces[i : i + 2]) if i + 1 < len(pieces) else pieces[i] for i in range(0, len(pieces), 2)]
    return jnp.max(pieces[0], axis=1, keepdims=True)


def weigh(scores, values, top):
    weights = jnp.exp2((scores - top) * TO_LOG2).astype(jnp.bfloat16)
    return jnp.dot(weights, values, preferred_element_type=jnp.float32)


def beside_ones(values, both_ref):
    head_dim = values.shape[1]
    both_ref[:, :head_dim] = values
    both_ref[:, head_dim:] = jnp.ones_like(values)


def block_of(ref, side, kind):
    rows = ref.shape[0] * ref.shape[2] * ref.shape[4]
    return ref[:, side, :, kind].reshape(rows, ref.shape[5])


def first_kernel(pos_ref, q_ref, start_ref, held_ref, mixed_ref, log_ref, starts_ref, row_ref, own_ref, far_ref, sem):
    span, head_dim = q_ref.shape
    pos = pos_ref[0]
    side = lax.rem(pos // 2, 2)
    fetch = pltpu.make_async_copy(start_ref, row_ref, sem)
    fetch.start()
    own_keys, far_keys = block_of(held_ref, side, 0), block_of(held_ref, 1 - side, 0)

    def products_of(r):
        rows = slice(r * ROWS, (r + 1) * ROWS)
        q = q_ref[rows, :]
        past = dot_nt(q, own_keys[: r * ROWS]) if r else None
        return dot_nt(q, own_keys[rows]), past, dot_nt(q, far_keys)

    upcoming = products_of(0)
    beside_ones(block_of(held_ref, side, 1), own_ref)
    beside_ones(block_of(held_ref, 1 - side, 1), far_ref)
    fetch.wait()
    starts_ref[...] = jnp.broadcast_to(row_ref[...], (head_dim, span)).T
    for r in range(span // ROWS):
        rows = slice(r * ROWS, (r + 1) * ROWS)
        near, past, far = upcoming
        if (r + 1) * ROWS < span:
            upcoming = products_of(r + 1)
        starts = starts_ref[rows, :1]
        query_pos = pos * span + r * ROWS + lax.broadcasted_iota(jnp.int32, (ROWS, 1), 0)
        parts = [
            (hide(near, pos * span + r * ROWS, starts, query_pos), own_ref[rows, :]),
            (hide(far, (pos - 2) * span, starts), far_ref[...]),
        ]
        if r:
            parts.append((hide(past, pos * span, starts), own_ref[: r * ROWS, :]))
        top = top_of(*[scores for scores, _ in parts])
        sums = sum(weigh(scores, values, top) for scores, values in parts)
        total = sums[:, head_dim:]
        mixed_ref[rows, :] = sums[:, :head_dim] / total
        log_ref[rows, :] = top * TO_LOG2 + jnp.log2(total)


def second_kernel(pos_ref, q_ref, starts_ref, other_ref, mixed_ref, log_ref, out_ref, lse_ref, both_ref, out_vmem, lse_vmem, sems):
    span, head_dim = q_ref.shape
    pos = pos_ref[0]
    side, odd = lax.rem(pos // 2, 2), lax.rem(pos, 2)
    side = jnp.where(odd == 1, side, 1 - side)
    keys = block_of(other_ref, side, 0)
    products = [dot_nt(q_ref[:ROWS, :], keys)]
    beside_ones(block_of(other_ref, side, 1), both_ref)
    sends = []
    for r in range(span // ROWS):
        rows = slice(r * ROWS, (r + 1) * ROWS)
        scores = hide(products.pop(0), (pos - 1) * span, starts_ref[rows, :1])
        if (r + 1) * ROWS < span:
            products.append(dot_nt(q_ref[(r + 1) * ROWS : (r + 2) * ROWS, :], keys))
        top = top_of(scores)
        sums = weigh(scores, both_ref[...], top)
        top = top * TO_LOG2
        logs = log_ref[rows, :]
        joint = jnp.maximum(logs, top)
        before, after = jnp.exp2(logs - joint), jnp.exp2(top - joint)
        total = sums[:, head_dim:] * after + before
        mixed = mixed_ref[rows, :] * before + sums[:, :head_dim] * after
        out_vmem[rows, :] = (mixed / total).astype(out_ref.dtype)
        sends.append(pltpu.make_async_copy(out_vmem.at[rows], out_ref.at[rows], sems.at[r]))
        sends[-1].start()
        lse_vmem[:, rows] = row_of((joint + jnp.log2(total)) * LN2)
    sends.append(pltpu.make_async_copy(lse_vmem, lse_ref, sems.at[span // ROWS]))
    sends[-1].start()
    for send in sends:
        send.wait()


def row_of(column):
    rows, lanes = column.shape
    at = lax.broadcasted_iota(jnp.int32, (lanes, lanes), 0) == lax.broadcasted_iota(jnp.int32, (lanes, lanes), 1)
    picked = [
        jnp.sum(jnp.where(at, column[i : i + lanes], 0.0), axis=0, keepdims=True) for i in range(0, rows, lanes)
    ]
    return jnp.concatenate(picked, axis=1)


def attend(pos, queries, doc_start, held, other):
    span, head_dim = queries.shape
    state = jax.ShapeDtypeStruct((span, head_dim), jnp.float32)
    params = pltpu.CompilerParams(vmem_limit_bytes=VMEM_LIMIT)
    both = pltpu.VMEM((span, 2 * head_dim), jnp.bfloat16)

    def cost(blocks):
        return pl.CostEstimate(
            flops=4 * blocks * span * span * head_dim,
            bytes_accessed=3 << 20,
            transcendentals=blocks * span * span,
        )

    mixed, logs, starts = pl.pallas_call(
        first_kernel,
        out_shape=(state, state, jax.ShapeDtypeStruct((span, head_dim), jnp.int32)),
        in_specs=[SMEM, VMEM, HBM, VMEM],
        out_specs=(VMEM, VMEM, VMEM),
        scratch_shapes=[pltpu.VMEM((1, span), jnp.int32), both, both, pltpu.SemaphoreType.DMA],
        compiler_params=params,
        cost_estimate=cost(2),
    )(pos, queries, doc_start.reshape(1, span), held)
    return pl.pallas_call(
        second_kernel,
        out_shape=(
            jax.ShapeDtypeStruct((span, head_dim), jnp.bfloat16),
            jax.ShapeDtypeStruct((1, span), jnp.float32),
        ),
        in_specs=[SMEM, VMEM, VMEM, VMEM, VMEM, VMEM],
        out_specs=(HBM, HBM),
        scratch_shapes=[
            both,
            pltpu.VMEM((span, head_dim), jnp.bfloat16),
            pltpu.VMEM((1, span), jnp.float32),
            pltpu.SemaphoreType.DMA((span // ROWS + 1,)),
        ],
        compiler_params=params,
        cost_estimate=cost(1),
    )(pos, queries, starts, other, mixed, logs)


def body(queries, keys, values, doc_start):
    span, (shard, head_dim) = doc_start.shape[0], keys.shape
    count, heads = lax.axis_size("seq"), lax.axis_size("head")
    pos = lax.axis_index("seq")
    width = heads // 2
    own = jnp.where(lax.broadcasted_iota(jnp.int32, (2, shard, head_dim), 0) == 0, keys[None], values[None])
    upward = [(i, i + 4) for i in range(count - 4) if i % 4 >= 2]
    below = lax.ppermute(own, "seq", upward)
    to_side = lax.broadcasted_iota(jnp.int32, (2, 2, width) + own.shape, 1)
    sent = jnp.where((to_side == 0) & (pos % 4 >= 2), below, own)
    slabs = [
        [(z * 4 + side * 2 + core) * heads + high * width + y for high in range(2) for side in range(2) for y in range(width)]
        for z in range(count // 4)
        for core in range(2)
    ]
    held = lax.all_to_all(sent.reshape((4 * width,) + own.shape), AXES, 0, 0, axis_index_groups=slabs)
    held = held.reshape(sent.shape)
    other = lax.ppermute(held, "seq", [(i, i ^ 1) for i in range(count)])
    return attend(jnp.stack([pos]).astype(jnp.int32), queries, doc_start, held, other)


def solution(mesh):
    in_specs = (P("seq", "head"), P(("seq", "head"), None), P(("seq", "head"), None), P("seq"))
    out_specs = (P("seq", "head"), P("head", "seq"))
    return jax.shard_map(body, mesh=mesh, in_specs=in_specs, out_specs=out_specs, check_vma=False)
```

```python
import math

import jax
import jax.numpy as jnp
from jax import lax
from jax.experimental import pallas as pl
from jax.experimental.pallas import tpu as pltpu
from jax.sharding import PartitionSpec as P

negative_fill = -1e30
ROWS = 256
VMEM = pl.BlockSpec(memory_space=pltpu.VMEM)
SMEM = pl.BlockSpec(memory_space=pltpu.SMEM)
HBM = pl.BlockSpec(memory_space=pltpu.HBM)
LN2 = math.log(2.0)
TOTAL_MAX = 2.0**100
VMEM_LIMIT = 32 * 1024 * 1024
HEAD_DIM = 128
TO_LOG2 = math.log2(math.e) / math.sqrt(HEAD_DIM)
AXES = ("seq", "head")


def dot_nt(a, b):
    return lax.dot_general(a, b, (((1,), (1,)), ((), ())), preferred_element_type=jnp.float32)


def hide(products, key_base, starts, query_pos=None):
    key_pos = key_base + lax.broadcasted_iota(jnp.int32, products.shape, 1)
    visible = key_pos >= starts
    if query_pos is not None:
        visible &= key_pos <= query_pos
    return jnp.where(visible, products, negative_fill)


def top_of(*parts, lanes=128):
    pieces = [scores[:, i : i + lanes] for scores in parts for i in range(0, scores.shape[1], lanes)]
    while len(pieces) > 1:
        pieces = [jnp.maximum(*pieces[i : i + 2]) if i + 1 < len(pieces) else pieces[i] for i in range(0, len(pieces), 2)]
    return jnp.max(pieces[0], axis=1, keepdims=True)


def weigh(scores, values, shift):
    wide = jnp.concatenate([shift] * (scores.shape[1] // shift.shape[1]), axis=1) if shift.shape[1] > 1 else shift
    weights = jnp.exp2(scores * TO_LOG2 - wide).astype(jnp.bfloat16)
    return jnp.dot(weights, values, preferred_element_type=jnp.float32)


def beside_ones(values, both_ref):
    head_dim = values.shape[1]
    both_ref[:, :head_dim] = values
    both_ref[:, head_dim:] = jnp.ones_like(values)


def block_of(ref, side, kind):
    rows = ref.shape[0] * ref.shape[2] * ref.shape[4]
    return ref[:, side, :, kind].reshape(rows, ref.shape[5])


def query_positions(pos, r, span):
    return pos * span + r * ROWS + lax.broadcasted_iota(jnp.int32, (ROWS, 1), 0)


def products_of(r, q_ref, own_keys, far_keys):
    rows = slice(r * ROWS, (r + 1) * ROWS)
    q = q_ref[rows, :]
    past = dot_nt(q, own_keys[: r * ROWS]) if r else None
    return dot_nt(q, own_keys[rows]), past, dot_nt(q, far_keys)


def parts_of(r, pos, products, starts, own_ref, far_ref):
    rows, span = slice(r * ROWS, (r + 1) * ROWS), far_ref.shape[0]
    near, past, far = products
    parts = [(hide(far, (pos - 2) * span, starts), far_ref[...])]
    if r:
        parts.append((hide(past, pos * span, starts), own_ref[: r * ROWS, :]))
    parts.append((hide(near, pos * span + r * ROWS, starts, query_positions(pos, r, span)), own_ref[rows, :]))
    return parts


def first_kernel(pos_ref, q_ref, start_ref, held_ref, mixed_ref, log_ref, starts_ref, row_ref, own_ref, far_ref, sem):
    span, head_dim = q_ref.shape
    pos = pos_ref[0]
    side = lax.rem(pos // 2, 2)
    fetch = pltpu.make_async_copy(start_ref, row_ref, sem)
    fetch.start()
    own_keys, far_keys = block_of(held_ref, side, 0), block_of(held_ref, 1 - side, 0)
    upcoming = products_of(0, q_ref, own_keys, far_keys)
    beside_ones(block_of(held_ref, side, 1), own_ref)
    beside_ones(block_of(held_ref, 1 - side, 1), far_ref)
    with_own = jnp.sum(q_ref[...].astype(jnp.float32) * own_keys.astype(jnp.float32), axis=1, keepdims=True)
    log_ref[...] = jnp.broadcast_to(with_own * TO_LOG2, log_ref.shape)
    fetch.wait()
    starts_ref[...] = jnp.broadcast_to(row_ref[...], (head_dim, span)).T
    for r in range(span // ROWS):
        rows = slice(r * ROWS, (r + 1) * ROWS)
        products = upcoming
        if (r + 1) * ROWS < span:
            upcoming = products_of(r + 1, q_ref, own_keys, far_keys)
        shift = log_ref[rows, :]
        parts = parts_of(r, pos, products, starts_ref[rows, :1], own_ref, far_ref)
        sums = sum(weigh(scores, values, shift[:, :1]) for scores, values in parts)
        total = sums[:, head_dim:]
        mixed_ref[rows, :] = sums[:, :head_dim] / total
        log_ref[rows, :] = jnp.where(total <= TOTAL_MAX, shift + jnp.log2(total), -jnp.inf)


def second_kernel(
    pos_ref, q_ref, starts_ref, held_ref, other_ref, mixed_ref, log_ref, out_ref, lse_ref, both_ref, own_ref, far_ref, out_vmem, lse_vmem, sems
):
    span, head_dim = q_ref.shape
    pos = pos_ref[0]
    own_side, odd = lax.rem(pos // 2, 2), lax.rem(pos, 2)
    side = jnp.where(odd == 1, own_side, 1 - own_side)
    keys = block_of(other_ref, side, 0)
    tiles = span // ROWS

    def products_with(r):
        return dot_nt(q_ref[r * ROWS : (r + 1) * ROWS, :], keys)

    def scores_of(r, products):
        return hide(products, (pos - 1) * span, starts_ref[r * ROWS : (r + 1) * ROWS, :1])

    def send(r):
        rows = slice(r * ROWS, (r + 1) * ROWS)
        return pltpu.make_async_copy(out_vmem.at[rows], out_ref.at[rows], sems.at[r])

    send_lse = pltpu.make_async_copy(lse_vmem, lse_ref, sems.at[tiles])

    def finish(r, mixed, total, shift):
        rows = slice(r * ROWS, (r + 1) * ROWS)
        out_vmem[rows, :] = (mixed / total).astype(out_ref.dtype)
        send(r).start()
        lse_vmem[:, rows] = row_of((shift + jnp.log2(total)) * LN2)

    def end():
        for r in range(tiles):
            send(r).wait()
        send_lse.wait()

    beside_ones(block_of(other_ref, side, 1), both_ref)
    largest = None
    for r in range(tiles):
        rows = slice(r * ROWS, (r + 1) * ROWS)
        products = products_with(r)
        logs = log_ref[rows, :]
        sums = weigh(scores_of(r, products), both_ref[...], logs)
        total = sums[:, head_dim:] + 1.0
        finish(r, mixed_ref[rows, :] + sums[:, :head_dim], total, logs)
        largest = total if r == 0 else jnp.maximum(largest, total)
    send_lse.start()
    again = jnp.logical_not(jnp.max(largest) <= TOTAL_MAX)
    end()

    @pl.when(again)
    def _():
        own_keys, far_keys = block_of(held_ref, own_side, 0), block_of(held_ref, 1 - own_side, 0)
        beside_ones(block_of(held_ref, own_side, 1), own_ref)
        beside_ones(block_of(held_ref, 1 - own_side, 1), far_ref)
        for r in range(tiles):
            products = products_of(r, q_ref, own_keys, far_keys)
            parts = parts_of(r, pos, products, starts_ref[r * ROWS : (r + 1) * ROWS, :1], own_ref, far_ref)
            parts.append((scores_of(r, products_with(r)), both_ref[...]))
            shift = top_of(*[scores for scores, _ in parts]) * TO_LOG2
            sums = sum(weigh(scores, values, shift) for scores, values in parts)
            finish(r, sums[:, :head_dim], sums[:, head_dim:], shift)
        send_lse.start()
        end()


def row_of(column):
    rows, lanes = column.shape
    at = lax.broadcasted_iota(jnp.int32, (lanes, lanes), 0) == lax.broadcasted_iota(jnp.int32, (lanes, lanes), 1)
    picked = [
        jnp.sum(jnp.where(at, column[i : i + lanes], 0.0), axis=0, keepdims=True) for i in range(0, rows, lanes)
    ]
    return jnp.concatenate(picked, axis=1)


def attend(pos, queries, doc_start, held, other):
    span, head_dim = queries.shape
    state = jax.ShapeDtypeStruct((span, head_dim), jnp.float32)
    params = pltpu.CompilerParams(vmem_limit_bytes=VMEM_LIMIT)
    both = pltpu.VMEM((span, 2 * head_dim), jnp.bfloat16)

    def cost(blocks):
        return pl.CostEstimate(
            flops=4 * blocks * span * span * head_dim,
            bytes_accessed=3 << 20,
            transcendentals=blocks * span * span,
        )

    mixed, logs, starts = pl.pallas_call(
        first_kernel,
        out_shape=(state, state, jax.ShapeDtypeStruct((span, head_dim), jnp.int32)),
        in_specs=[SMEM, VMEM, HBM, VMEM],
        out_specs=(VMEM, VMEM, VMEM),
        scratch_shapes=[pltpu.VMEM((1, span), jnp.int32), both, both, pltpu.SemaphoreType.DMA],
        compiler_params=params,
        cost_estimate=cost(2),
    )(pos, queries, doc_start.reshape(1, span), held)
    return pl.pallas_call(
        second_kernel,
        out_shape=(
            jax.ShapeDtypeStruct((span, head_dim), jnp.bfloat16),
            jax.ShapeDtypeStruct((1, span), jnp.float32),
        ),
        in_specs=[SMEM, VMEM, VMEM, VMEM, VMEM, VMEM, VMEM],
        out_specs=(HBM, HBM),
        scratch_shapes=[
            both,
            both,
            both,
            pltpu.VMEM((span, head_dim), jnp.bfloat16),
            pltpu.VMEM((1, span), jnp.float32),
            pltpu.SemaphoreType.DMA((span // ROWS + 1,)),
        ],
        compiler_params=params,
        cost_estimate=cost(1),
    )(pos, queries, starts, held, other, mixed, logs)


def body(queries, keys, values, doc_start):
    span, (shard, head_dim) = doc_start.shape[0], keys.shape
    count, heads = lax.axis_size("seq"), lax.axis_size("head")
    pos = lax.axis_index("seq")
    width = heads // 2
    own = jnp.where(lax.broadcasted_iota(jnp.int32, (2, shard, head_dim), 0) == 0, keys[None], values[None])
    upward = [(i, i + 4) for i in range(count - 4) if i % 4 >= 2]
    below = lax.ppermute(own, "seq", upward)
    to_side = lax.broadcasted_iota(jnp.int32, (2, 2, width) + own.shape, 1)
    sent = jnp.where((to_side == 0) & (pos % 4 >= 2), below, own)
    slabs = [
        [(z * 4 + side * 2 + core) * heads + high * width + y for high in range(2) for side in range(2) for y in range(width)]
        for z in range(count // 4)
        for core in range(2)
    ]
    held = lax.all_to_all(sent.reshape((4 * width,) + own.shape), AXES, 0, 0, axis_index_groups=slabs)
    held = held.reshape(sent.shape)
    other = lax.ppermute(held, "seq", [(i, i ^ 1) for i in range(count)])
    return attend(jnp.stack([pos]).astype(jnp.int32), queries, doc_start, held, other)


def solution(mesh):
    in_specs = (P("seq", "head"), P(("seq", "head"), None), P(("seq", "head"), None), P("seq"))
    out_specs = (P("seq", "head"), P("head", "seq"))
    return jax.shard_map(body, mesh=mesh, in_specs=in_specs, out_specs=out_specs, check_vma=False)
```

```python
import math

import jax
import jax.numpy as jnp
from jax import lax
from jax.experimental import pallas as pl
from jax.experimental.pallas import tpu as pltpu
from jax.sharding import PartitionSpec as P

negative_fill = -1e30
ROWS = 256
VMEM = pl.BlockSpec(memory_space=pltpu.VMEM)
SMEM = pl.BlockSpec(memory_space=pltpu.SMEM)
HBM = pl.BlockSpec(memory_space=pltpu.HBM)
LN2 = math.log(2.0)
TOTAL_MAX = 2.0**100
VMEM_LIMIT = 32 * 1024 * 1024
HEAD_DIM = 128
TO_LOG2 = math.log2(math.e) / math.sqrt(HEAD_DIM)
AXES = ("seq", "head")


def dot_nt(a, b):
    return lax.dot_general(a, b, (((1,), (1,)), ((), ())), preferred_element_type=jnp.float32)


def hide(products, key_base, starts, query_pos=None):
    key_pos = key_base + lax.broadcasted_iota(jnp.int32, products.shape, 1)
    visible = key_pos >= starts
    if query_pos is not None:
        visible &= key_pos <= query_pos
    return jnp.where(visible, products, negative_fill)


def top_of(*parts, lanes=128):
    pieces = [scores[:, i : i + lanes] for scores in parts for i in range(0, scores.shape[1], lanes)]
    while len(pieces) > 1:
        pieces = [jnp.maximum(*pieces[i : i + 2]) if i + 1 < len(pieces) else pieces[i] for i in range(0, len(pieces), 2)]
    return jnp.max(pieces[0], axis=1, keepdims=True)


def weigh(scores, values, shift):
    wide = jnp.concatenate([shift] * (scores.shape[1] // shift.shape[1]), axis=1) if shift.shape[1] > 1 else shift
    weights = jnp.exp2(scores * TO_LOG2 - wide).astype(jnp.bfloat16)
    return jnp.dot(weights, values, preferred_element_type=jnp.float32)


def beside_ones(values, both_ref):
    head_dim = values.shape[1]
    both_ref[:, :head_dim] = values
    both_ref[:, head_dim:] = jnp.ones_like(values)


def block_of(ref, side, kind):
    highs, width = ref.shape[0], ref.shape[2]
    half = width // 2
    at = [y + side * (half if y < half else -half) for y in range(width)]
    return jnp.concatenate([ref[high, side, at[y], kind] for high in range(highs) for y in range(width)], axis=0)


def query_positions(pos, r, span):
    return pos * span + r * ROWS + lax.broadcasted_iota(jnp.int32, (ROWS, 1), 0)


def products_of(r, q_ref, own_keys, far_keys):
    rows = slice(r * ROWS, (r + 1) * ROWS)
    q = q_ref[rows, :]
    past = dot_nt(q, own_keys[: r * ROWS]) if r else None
    return dot_nt(q, own_keys[rows]), past, dot_nt(q, far_keys)


def parts_of(r, pos, products, starts, own_ref, far_ref):
    rows, span = slice(r * ROWS, (r + 1) * ROWS), far_ref.shape[0]
    near, past, far = products
    parts = [(hide(far, (pos - 2) * span, starts), far_ref[...])]
    if r:
        parts.append((hide(past, pos * span, starts), own_ref[: r * ROWS, :]))
    parts.append((hide(near, pos * span + r * ROWS, starts, query_positions(pos, r, span)), own_ref[rows, :]))
    return parts


def first_kernel(pos_ref, q_ref, start_ref, held_ref, mixed_ref, log_ref, starts_ref, row_ref, own_ref, far_ref, sem):
    span, head_dim = q_ref.shape
    pos = pos_ref[0]
    side = lax.rem(pos // 2, 2)
    fetch = pltpu.make_async_copy(start_ref, row_ref, sem)
    fetch.start()
    own_keys, far_keys = block_of(held_ref, side, 0), block_of(held_ref, 1 - side, 0)
    upcoming = products_of(0, q_ref, own_keys, far_keys)
    beside_ones(block_of(held_ref, side, 1), own_ref)
    beside_ones(block_of(held_ref, 1 - side, 1), far_ref)
    with_own = jnp.sum(q_ref[...].astype(jnp.float32) * own_keys.astype(jnp.float32), axis=1, keepdims=True)
    log_ref[...] = jnp.broadcast_to(with_own * TO_LOG2, log_ref.shape)
    fetch.wait()
    starts_ref[...] = jnp.broadcast_to(row_ref[...], (head_dim, span)).T
    for r in range(span // ROWS):
        rows = slice(r * ROWS, (r + 1) * ROWS)
        products = upcoming
        if (r + 1) * ROWS < span:
            upcoming = products_of(r + 1, q_ref, own_keys, far_keys)
        shift = log_ref[rows, :]
        parts = parts_of(r, pos, products, starts_ref[rows, :1], own_ref, far_ref)
        sums = sum(weigh(scores, values, shift[:, :1]) for scores, values in parts)
        total = sums[:, head_dim:]
        mixed_ref[rows, :] = sums[:, :head_dim] / total
        log_ref[rows, :] = jnp.where(total <= TOTAL_MAX, shift + jnp.log2(total), -jnp.inf)


def second_kernel(
    pos_ref, q_ref, starts_ref, held_ref, other_ref, mixed_ref, log_ref, out_ref, lse_ref, both_ref, own_ref, far_ref, out_vmem, lse_vmem, sems
):
    span, head_dim = q_ref.shape
    pos = pos_ref[0]
    own_side, odd = lax.rem(pos // 2, 2), lax.rem(pos, 2)
    side = jnp.where(odd == 1, own_side, 1 - own_side)
    keys = block_of(other_ref, side, 0)
    tiles = span // ROWS

    def products_with(r):
        return dot_nt(q_ref[r * ROWS : (r + 1) * ROWS, :], keys)

    def scores_of(r, products):
        return hide(products, (pos - 1) * span, starts_ref[r * ROWS : (r + 1) * ROWS, :1])

    def send(r):
        rows = slice(r * ROWS, (r + 1) * ROWS)
        return pltpu.make_async_copy(out_vmem.at[rows], out_ref.at[rows], sems.at[r])

    send_lse = pltpu.make_async_copy(lse_vmem, lse_ref, sems.at[tiles])

    def finish(r, mixed, total, shift):
        rows = slice(r * ROWS, (r + 1) * ROWS)
        out_vmem[rows, :] = (mixed / total).astype(out_ref.dtype)
        send(r).start()
        lse_vmem[:, rows] = row_of((shift + jnp.log2(total)) * LN2)

    def end():
        for r in range(tiles):
            send(r).wait()
        send_lse.wait()

    beside_ones(block_of(other_ref, side, 1), both_ref)
    largest = None
    for r in range(tiles):
        rows = slice(r * ROWS, (r + 1) * ROWS)
        products = products_with(r)
        logs = log_ref[rows, :]
        sums = weigh(scores_of(r, products), both_ref[...], logs)
        total = sums[:, head_dim:] + 1.0
        finish(r, mixed_ref[rows, :] + sums[:, :head_dim], total, logs)
        largest = total if r == 0 else jnp.maximum(largest, total)
    send_lse.start()
    again = jnp.logical_not(jnp.max(largest) <= TOTAL_MAX)
    end()

    @pl.when(again)
    def _():
        own_keys, far_keys = block_of(held_ref, own_side, 0), block_of(held_ref, 1 - own_side, 0)
        beside_ones(block_of(held_ref, own_side, 1), own_ref)
        beside_ones(block_of(held_ref, 1 - own_side, 1), far_ref)
        for r in range(tiles):
            products = products_of(r, q_ref, own_keys, far_keys)
            parts = parts_of(r, pos, products, starts_ref[r * ROWS : (r + 1) * ROWS, :1], own_ref, far_ref)
            parts.append((scores_of(r, products_with(r)), both_ref[...]))
            shift = top_of(*[scores for scores, _ in parts]) * TO_LOG2
            sums = sum(weigh(scores, values, shift) for scores, values in parts)
            finish(r, sums[:, :head_dim], sums[:, head_dim:], shift)
        send_lse.start()
        end()


def row_of(column):
    rows, lanes = column.shape
    at = lax.broadcasted_iota(jnp.int32, (lanes, lanes), 0) == lax.broadcasted_iota(jnp.int32, (lanes, lanes), 1)
    picked = [
        jnp.sum(jnp.where(at, column[i : i + lanes], 0.0), axis=0, keepdims=True) for i in range(0, rows, lanes)
    ]
    return jnp.concatenate(picked, axis=1)


def attend(pos, queries, doc_start, held, other):
    span, head_dim = queries.shape
    state = jax.ShapeDtypeStruct((span, head_dim), jnp.float32)
    params = pltpu.CompilerParams(vmem_limit_bytes=VMEM_LIMIT)
    both = pltpu.VMEM((span, 2 * head_dim), jnp.bfloat16)

    def cost(blocks):
        return pl.CostEstimate(
            flops=4 * blocks * span * span * head_dim,
            bytes_accessed=3 << 20,
            transcendentals=blocks * span * span,
        )

    mixed, logs, starts = pl.pallas_call(
        first_kernel,
        out_shape=(state, state, jax.ShapeDtypeStruct((span, head_dim), jnp.int32)),
        in_specs=[SMEM, VMEM, HBM, VMEM],
        out_specs=(VMEM, VMEM, VMEM),
        scratch_shapes=[pltpu.VMEM((1, span), jnp.int32), both, both, pltpu.SemaphoreType.DMA],
        compiler_params=params,
        cost_estimate=cost(2),
    )(pos, queries, doc_start.reshape(1, span), held)
    return pl.pallas_call(
        second_kernel,
        out_shape=(
            jax.ShapeDtypeStruct((span, head_dim), jnp.bfloat16),
            jax.ShapeDtypeStruct((1, span), jnp.float32),
        ),
        in_specs=[SMEM, VMEM, VMEM, VMEM, VMEM, VMEM, VMEM],
        out_specs=(HBM, HBM),
        scratch_shapes=[
            both,
            both,
            both,
            pltpu.VMEM((span, head_dim), jnp.bfloat16),
            pltpu.VMEM((1, span), jnp.float32),
            pltpu.SemaphoreType.DMA((span // ROWS + 1,)),
        ],
        compiler_params=params,
        cost_estimate=cost(1),
    )(pos, queries, starts, held, other, mixed, logs)


def body(queries, keys, values, doc_start):
    span, (shard, head_dim) = doc_start.shape[0], keys.shape
    count, heads = lax.axis_size("seq"), lax.axis_size("head")
    pos = lax.axis_index("seq")
    width = heads // 2
    own = jnp.where(lax.broadcasted_iota(jnp.int32, (2, shard, head_dim), 0) == 0, keys[None], values[None])
    upward = [(i, i + 4) for i in range(count - 4) if i % 4 >= 2]
    below = lax.ppermute(own, "seq", upward)
    to_side = lax.broadcasted_iota(jnp.int32, (2, 2, width) + own.shape, 1)
    sent = jnp.where((to_side == 0) & (pos % 4 >= 2), below, own)
    slabs = [
        [
            (z * 4 + side * 2 + core) * heads + high * width + (y + side * (width // 2)) % width
            for high in range(2)
            for side in range(2)
            for y in range(width)
        ]
        for z in range(count // 4)
        for core in range(2)
    ]
    held = lax.all_to_all(sent.reshape((4 * width,) + own.shape), AXES, 0, 0, axis_index_groups=slabs)
    held = held.reshape(sent.shape)
    other = lax.ppermute(held, "seq", [(i, i ^ 1) for i in range(count)])
    return attend(jnp.stack([pos]).astype(jnp.int32), queries, doc_start, held, other)


def solution(mesh):
    in_specs = (P("seq", "head"), P(("seq", "head"), None), P(("seq", "head"), None), P("seq"))
    out_specs = (P("seq", "head"), P("head", "seq"))
    return jax.shard_map(body, mesh=mesh, in_specs=in_specs, out_specs=out_specs, check_vma=False)
```

```python
import math

import jax
import jax.numpy as jnp
from jax import lax
from jax.experimental import pallas as pl
from jax.experimental.pallas import tpu as pltpu
from jax.sharding import PartitionSpec as P

negative_fill = -1e30
ROWS = 256
VMEM = pl.BlockSpec(memory_space=pltpu.VMEM)
SMEM = pl.BlockSpec(memory_space=pltpu.SMEM)
HBM = pl.BlockSpec(memory_space=pltpu.HBM)
LN2 = math.log(2.0)
TOTAL_MAX = 2.0**100
VMEM_LIMIT = 32 * 1024 * 1024
HEAD_DIM = 128
TO_LOG2 = math.log2(math.e) / math.sqrt(HEAD_DIM)
AXES = ("seq", "head")


def dot_nt(a, b):
    return lax.dot_general(a, b, (((1,), (1,)), ((), ())), preferred_element_type=jnp.float32)


def hide(products, key_base, starts, query_pos=None):
    key_pos = key_base + lax.broadcasted_iota(jnp.int32, products.shape, 1)
    visible = key_pos >= starts
    if query_pos is not None:
        visible &= key_pos <= query_pos
    return jnp.where(visible, products, negative_fill)


def top_of(*parts, lanes=128):
    pieces = [scores[:, i : i + lanes] for scores in parts for i in range(0, scores.shape[1], lanes)]
    while len(pieces) > 1:
        pieces = [jnp.maximum(*pieces[i : i + 2]) if i + 1 < len(pieces) else pieces[i] for i in range(0, len(pieces), 2)]
    return jnp.max(pieces[0], axis=1, keepdims=True)


def weigh(scores, values, shift):
    wide = jnp.concatenate([shift] * (scores.shape[1] // shift.shape[1]), axis=1) if shift.shape[1] > 1 else shift
    weights = jnp.exp2(scores * TO_LOG2 - wide).astype(jnp.bfloat16)
    return jnp.dot(weights, values, preferred_element_type=jnp.float32)


def beside_ones(values, both_ref):
    head_dim = values.shape[1]
    both_ref[:, :head_dim] = values
    both_ref[:, head_dim:] = jnp.ones_like(values)


def block_of(ref, side, kind, core):
    highs, width = ref.shape[0], ref.shape[2]
    half = width // 2
    turned = lax.rem(side + core, 2)
    at = [y + turned * (half if y < half else -half) for y in range(width)]
    return jnp.concatenate([ref[high, side, at[y], kind] for high in range(highs) for y in range(width)], axis=0)


def query_positions(pos, r, span):
    return pos * span + r * ROWS + lax.broadcasted_iota(jnp.int32, (ROWS, 1), 0)


def products_of(r, q_ref, own_keys, far_keys):
    rows = slice(r * ROWS, (r + 1) * ROWS)
    q = q_ref[rows, :]
    past = dot_nt(q, own_keys[: r * ROWS]) if r else None
    return dot_nt(q, own_keys[rows]), past, dot_nt(q, far_keys)


def parts_of(r, pos, products, starts, own_ref, far_ref):
    rows, span = slice(r * ROWS, (r + 1) * ROWS), far_ref.shape[0]
    near, past, far = products
    parts = [(hide(far, (pos - 2) * span, starts), far_ref[...])]
    if r:
        parts.append((hide(past, pos * span, starts), own_ref[: r * ROWS, :]))
    parts.append((hide(near, pos * span + r * ROWS, starts, query_positions(pos, r, span)), own_ref[rows, :]))
    return parts


def first_kernel(pos_ref, q_ref, start_ref, held_ref, mixed_ref, log_ref, starts_ref, row_ref, own_ref, far_ref, sem):
    span, head_dim = q_ref.shape
    pos = pos_ref[0]
    side, core = lax.rem(pos // 2, 2), lax.rem(pos, 2)
    fetch = pltpu.make_async_copy(start_ref, row_ref, sem)
    fetch.start()
    own_keys, far_keys = block_of(held_ref, side, 0, core), block_of(held_ref, 1 - side, 0, core)
    upcoming = products_of(0, q_ref, own_keys, far_keys)
    beside_ones(block_of(held_ref, side, 1, core), own_ref)
    beside_ones(block_of(held_ref, 1 - side, 1, core), far_ref)
    with_own = jnp.sum(q_ref[...].astype(jnp.float32) * own_keys.astype(jnp.float32), axis=1, keepdims=True)
    log_ref[...] = jnp.broadcast_to(with_own * TO_LOG2, log_ref.shape)
    fetch.wait()
    starts_ref[...] = jnp.broadcast_to(row_ref[...], (head_dim, span)).T
    for r in range(span // ROWS):
        rows = slice(r * ROWS, (r + 1) * ROWS)
        products = upcoming
        if (r + 1) * ROWS < span:
            upcoming = products_of(r + 1, q_ref, own_keys, far_keys)
        shift = log_ref[rows, :]
        parts = parts_of(r, pos, products, starts_ref[rows, :1], own_ref, far_ref)
        sums = sum(weigh(scores, values, shift[:, :1]) for scores, values in parts)
        total = sums[:, head_dim:]
        mixed_ref[rows, :] = sums[:, :head_dim] / total
        log_ref[rows, :] = jnp.where(total <= TOTAL_MAX, shift + jnp.log2(total), -jnp.inf)


def second_kernel(
    pos_ref, q_ref, starts_ref, held_ref, other_ref, mixed_ref, log_ref, out_ref, lse_ref, both_ref, own_ref, far_ref, out_vmem, lse_vmem, sems
):
    span, head_dim = q_ref.shape
    pos = pos_ref[0]
    own_side, odd = lax.rem(pos // 2, 2), lax.rem(pos, 2)
    side = jnp.where(odd == 1, own_side, 1 - own_side)
    keys = block_of(other_ref, side, 0, 1 - odd)
    tiles = span // ROWS

    def products_with(r):
        return dot_nt(q_ref[r * ROWS : (r + 1) * ROWS, :], keys)

    def scores_of(r, products):
        return hide(products, (pos - 1) * span, starts_ref[r * ROWS : (r + 1) * ROWS, :1])

    def send(r):
        rows = slice(r * ROWS, (r + 1) * ROWS)
        return pltpu.make_async_copy(out_vmem.at[rows], out_ref.at[rows], sems.at[r])

    send_lse = pltpu.make_async_copy(lse_vmem, lse_ref, sems.at[tiles])

    def finish(r, mixed, total, shift):
        rows = slice(r * ROWS, (r + 1) * ROWS)
        out_vmem[rows, :] = (mixed / total).astype(out_ref.dtype)
        send(r).start()
        lse_vmem[:, rows] = row_of((shift + jnp.log2(total)) * LN2)

    def end():
        for r in range(tiles):
            send(r).wait()
        send_lse.wait()

    beside_ones(block_of(other_ref, side, 1, 1 - odd), both_ref)
    largest = None
    for r in range(tiles):
        rows = slice(r * ROWS, (r + 1) * ROWS)
        products = products_with(r)
        logs = log_ref[rows, :]
        sums = weigh(scores_of(r, products), both_ref[...], logs)
        total = sums[:, head_dim:] + 1.0
        finish(r, mixed_ref[rows, :] + sums[:, :head_dim], total, logs)
        largest = total if r == 0 else jnp.maximum(largest, total)
    send_lse.start()
    again = jnp.logical_not(jnp.max(largest) <= TOTAL_MAX)
    end()

    @pl.when(again)
    def _():
        own_keys, far_keys = block_of(held_ref, own_side, 0, odd), block_of(held_ref, 1 - own_side, 0, odd)
        beside_ones(block_of(held_ref, own_side, 1, odd), own_ref)
        beside_ones(block_of(held_ref, 1 - own_side, 1, odd), far_ref)
        for r in range(tiles):
            products = products_of(r, q_ref, own_keys, far_keys)
            parts = parts_of(r, pos, products, starts_ref[r * ROWS : (r + 1) * ROWS, :1], own_ref, far_ref)
            parts.append((scores_of(r, products_with(r)), both_ref[...]))
            shift = top_of(*[scores for scores, _ in parts]) * TO_LOG2
            sums = sum(weigh(scores, values, shift) for scores, values in parts)
            finish(r, sums[:, :head_dim], sums[:, head_dim:], shift)
        send_lse.start()
        end()


def row_of(column):
    rows, lanes = column.shape
    at = lax.broadcasted_iota(jnp.int32, (lanes, lanes), 0) == lax.broadcasted_iota(jnp.int32, (lanes, lanes), 1)
    picked = [
        jnp.sum(jnp.where(at, column[i : i + lanes], 0.0), axis=0, keepdims=True) for i in range(0, rows, lanes)
    ]
    return jnp.concatenate(picked, axis=1)


def attend(pos, queries, doc_start, held, other):
    span, head_dim = queries.shape
    state = jax.ShapeDtypeStruct((span, head_dim), jnp.float32)
    params = pltpu.CompilerParams(vmem_limit_bytes=VMEM_LIMIT)
    both = pltpu.VMEM((span, 2 * head_dim), jnp.bfloat16)

    def cost(blocks):
        return pl.CostEstimate(
            flops=4 * blocks * span * span * head_dim,
            bytes_accessed=3 << 20,
            transcendentals=blocks * span * span,
        )

    mixed, logs, starts = pl.pallas_call(
        first_kernel,
        out_shape=(state, state, jax.ShapeDtypeStruct((span, head_dim), jnp.int32)),
        in_specs=[SMEM, VMEM, HBM, VMEM],
        out_specs=(VMEM, VMEM, VMEM),
        scratch_shapes=[pltpu.VMEM((1, span), jnp.int32), both, both, pltpu.SemaphoreType.DMA],
        compiler_params=params,
        cost_estimate=cost(2),
    )(pos, queries, doc_start.reshape(1, span), held)
    return pl.pallas_call(
        second_kernel,
        out_shape=(
            jax.ShapeDtypeStruct((span, head_dim), jnp.bfloat16),
            jax.ShapeDtypeStruct((1, span), jnp.float32),
        ),
        in_specs=[SMEM, VMEM, VMEM, VMEM, VMEM, VMEM, VMEM],
        out_specs=(HBM, HBM),
        scratch_shapes=[
            both,
            both,
            both,
            pltpu.VMEM((span, head_dim), jnp.bfloat16),
            pltpu.VMEM((1, span), jnp.float32),
            pltpu.SemaphoreType.DMA((span // ROWS + 1,)),
        ],
        compiler_params=params,
        cost_estimate=cost(1),
    )(pos, queries, starts, held, other, mixed, logs)


def body(queries, keys, values, doc_start):
    span, (shard, head_dim) = doc_start.shape[0], keys.shape
    count, heads = lax.axis_size("seq"), lax.axis_size("head")
    pos = lax.axis_index("seq")
    width = heads // 2
    own = jnp.where(lax.broadcasted_iota(jnp.int32, (2, shard, head_dim), 0) == 0, keys[None], values[None])
    upward = [(i, i + 4) for i in range(count - 4) if i % 4 >= 2]
    below = lax.ppermute(own, "seq", upward)
    to_side = lax.broadcasted_iota(jnp.int32, (2, 2, width) + own.shape, 1)
    sent = jnp.where((to_side == 0) & (pos % 4 >= 2), below, own)
    slabs = [
        [
            (z * 4 + side * 2 + core) * heads + high * width + (y + (side + core) * (width // 2)) % width
            for high in range(2)
            for side in range(2)
            for y in range(width)
        ]
        for z in range(count // 4)
        for core in range(2)
    ]
    held = lax.all_to_all(sent.reshape((4 * width,) + own.shape), AXES, 0, 0, axis_index_groups=slabs)
    held = held.reshape(sent.shape)
    other = lax.ppermute(held, "seq", [(i, i ^ 1) for i in range(count)])
    return attend(jnp.stack([pos]).astype(jnp.int32), queries, doc_start, held, other)


def solution(mesh):
    in_specs = (P("seq", "head"), P(("seq", "head"), None), P(("seq", "head"), None), P("seq"))
    out_specs = (P("seq", "head"), P("head", "seq"))
    return jax.shard_map(body, mesh=mesh, in_specs=in_specs, out_specs=out_specs, check_vma=False)
```

```python
import math

import jax
import jax.numpy as jnp
from jax import lax
from jax.experimental import pallas as pl
from jax.experimental.pallas import tpu as pltpu
from jax.sharding import PartitionSpec as P

negative_fill = -1e30
ROWS = 256
VMEM = pl.BlockSpec(memory_space=pltpu.VMEM)
SMEM = pl.BlockSpec(memory_space=pltpu.SMEM)
HBM = pl.BlockSpec(memory_space=pltpu.HBM)
LN2 = math.log(2.0)
TOTAL_MAX = 2.0**100
VMEM_LIMIT = 32 * 1024 * 1024
HEAD_DIM = 128
TO_LOG2 = math.log2(math.e) / math.sqrt(HEAD_DIM)
AXES = ("seq", "head")


def dot_nt(a, b):
    return lax.dot_general(a, b, (((1,), (1,)), ((), ())), preferred_element_type=jnp.float32)


def hide(products, key_base, starts, query_pos=None):
    key_pos = key_base + lax.broadcasted_iota(jnp.int32, products.shape, 1)
    visible = key_pos >= starts
    if query_pos is not None:
        visible &= key_pos <= query_pos
    return jnp.where(visible, products, negative_fill)


def top_of(*parts, lanes=128):
    pieces = [scores[:, i : i + lanes] for scores in parts for i in range(0, scores.shape[1], lanes)]
    while len(pieces) > 1:
        pieces = [jnp.maximum(*pieces[i : i + 2]) if i + 1 < len(pieces) else pieces[i] for i in range(0, len(pieces), 2)]
    return jnp.max(pieces[0], axis=1, keepdims=True)


def weigh(scores, values, shift):
    wide = jnp.concatenate([shift] * (scores.shape[1] // shift.shape[1]), axis=1) if shift.shape[1] > 1 else shift
    weights = jnp.exp2(scores * TO_LOG2 - wide).astype(jnp.bfloat16)
    return jnp.dot(weights, values, preferred_element_type=jnp.float32)


def beside_ones(values, both_ref):
    head_dim = values.shape[1]
    both_ref[:, :head_dim] = values
    both_ref[:, head_dim:] = jnp.ones_like(values)


def block_of(ref, side, kind, core):
    highs, width = ref.shape[0], ref.shape[2]
    half = width // 2
    turned = lax.rem(side + core, 2)
    at = [y + turned * (half if y < half else -half) for y in range(width)]
    return jnp.concatenate([ref[high, side, at[y], kind] for high in range(highs) for y in range(width)], axis=0)


def query_positions(pos, r, span):
    return pos * span + r * ROWS + lax.broadcasted_iota(jnp.int32, (ROWS, 1), 0)


def products_of(r, q_ref, own_keys, far_keys):
    rows = slice(r * ROWS, (r + 1) * ROWS)
    q = q_ref[rows, :]
    past = dot_nt(q, own_keys[: r * ROWS]) if r else None
    return dot_nt(q, own_keys[rows]), past, dot_nt(q, far_keys)


def parts_of(r, pos, products, starts, own_ref, far_ref):
    rows, span = slice(r * ROWS, (r + 1) * ROWS), far_ref.shape[0]
    near, past, far = products
    parts = [(hide(far, (pos - 2) * span, starts), far_ref[...])]
    if r:
        parts.append((hide(past, pos * span, starts), own_ref[: r * ROWS, :]))
    parts.append((hide(near, pos * span + r * ROWS, starts, query_positions(pos, r, span)), own_ref[rows, :]))
    return parts


def first_kernel(pos_ref, q_ref, start_ref, held_ref, sums_ref, shift_ref, starts_ref, row_ref, own_ref, far_ref, sem):
    span, head_dim = q_ref.shape
    pos = pos_ref[0]
    side, core = lax.rem(pos // 2, 2), lax.rem(pos, 2)
    fetch = pltpu.make_async_copy(start_ref, row_ref, sem)
    fetch.start()
    own_keys, far_keys = block_of(held_ref, side, 0, core), block_of(held_ref, 1 - side, 0, core)
    upcoming = products_of(0, q_ref, own_keys, far_keys)
    beside_ones(block_of(held_ref, side, 1, core), own_ref)
    beside_ones(block_of(held_ref, 1 - side, 1, core), far_ref)
    with_own = jnp.sum(q_ref[...].astype(jnp.float32) * own_keys.astype(jnp.float32), axis=1, keepdims=True)
    shift_ref[...] = jnp.broadcast_to(with_own * TO_LOG2, shift_ref.shape)
    fetch.wait()
    starts_ref[...] = jnp.broadcast_to(row_ref[...], (head_dim, span)).T
    for r in range(span // ROWS):
        rows = slice(r * ROWS, (r + 1) * ROWS)
        products = upcoming
        if (r + 1) * ROWS < span:
            upcoming = products_of(r + 1, q_ref, own_keys, far_keys)
        shift = shift_ref[rows, :]
        parts = parts_of(r, pos, products, starts_ref[rows, :1], own_ref, far_ref)
        sums_ref[rows, :] = sum(weigh(scores, values, shift[:, :1]) for scores, values in parts)


def second_kernel(
    pos_ref, q_ref, starts_ref, held_ref, other_ref, sums_ref, shift_ref, out_ref, lse_ref, both_ref, own_ref, far_ref, out_vmem, lse_vmem, sems
):
    span, head_dim = q_ref.shape
    pos = pos_ref[0]
    own_side, odd = lax.rem(pos // 2, 2), lax.rem(pos, 2)
    side = jnp.where(odd == 1, own_side, 1 - own_side)
    keys = block_of(other_ref, side, 0, 1 - odd)
    tiles = span // ROWS

    def products_with(r):
        return dot_nt(q_ref[r * ROWS : (r + 1) * ROWS, :], keys)

    def scores_of(r, products):
        return hide(products, (pos - 1) * span, starts_ref[r * ROWS : (r + 1) * ROWS, :1])

    def send(r):
        rows = slice(r * ROWS, (r + 1) * ROWS)
        return pltpu.make_async_copy(out_vmem.at[rows], out_ref.at[rows], sems.at[r])

    send_lse = pltpu.make_async_copy(lse_vmem, lse_ref, sems.at[tiles])

    def finish(r, sums, shift):
        rows, total = slice(r * ROWS, (r + 1) * ROWS), sums[:, head_dim:]
        out_vmem[rows, :] = (sums[:, :head_dim] / total).astype(out_ref.dtype)
        send(r).start()
        lse_vmem[:, rows] = row_of((shift + jnp.log2(total)) * LN2)

    def end():
        for r in range(tiles):
            send(r).wait()
        send_lse.wait()

    beside_ones(block_of(other_ref, side, 1, 1 - odd), both_ref)
    largest = None
    for r in range(tiles):
        rows = slice(r * ROWS, (r + 1) * ROWS)
        products = products_with(r)
        shift = shift_ref[rows, :]
        sums = sums_ref[rows, :] + weigh(scores_of(r, products), both_ref[...], shift)
        finish(r, sums, shift)
        total = sums[:, head_dim:]
        largest = total if r == 0 else jnp.maximum(largest, total)
    send_lse.start()
    again = jnp.logical_not(jnp.max(largest) <= TOTAL_MAX)
    end()

    @pl.when(again)
    def _():
        own_keys, far_keys = block_of(held_ref, own_side, 0, odd), block_of(held_ref, 1 - own_side, 0, odd)
        beside_ones(block_of(held_ref, own_side, 1, odd), own_ref)
        beside_ones(block_of(held_ref, 1 - own_side, 1, odd), far_ref)
        for r in range(tiles):
            products = products_of(r, q_ref, own_keys, far_keys)
            parts = parts_of(r, pos, products, starts_ref[r * ROWS : (r + 1) * ROWS, :1], own_ref, far_ref)
            parts.append((scores_of(r, products_with(r)), both_ref[...]))
            shift = top_of(*[scores for scores, _ in parts]) * TO_LOG2
            sums = sum(weigh(scores, values, shift) for scores, values in parts)
            finish(r, sums, shift)
        send_lse.start()
        end()


def row_of(column):
    rows, lanes = column.shape
    at = lax.broadcasted_iota(jnp.int32, (lanes, lanes), 0) == lax.broadcasted_iota(jnp.int32, (lanes, lanes), 1)
    picked = [
        jnp.sum(jnp.where(at, column[i : i + lanes], 0.0), axis=0, keepdims=True) for i in range(0, rows, lanes)
    ]
    return jnp.concatenate(picked, axis=1)


def attend(pos, queries, doc_start, held, other):
    span, head_dim = queries.shape
    params = pltpu.CompilerParams(vmem_limit_bytes=VMEM_LIMIT)
    both = pltpu.VMEM((span, 2 * head_dim), jnp.bfloat16)

    def cost(blocks):
        return pl.CostEstimate(
            flops=4 * blocks * span * span * head_dim,
            bytes_accessed=3 << 20,
            transcendentals=blocks * span * span,
        )

    sums, shift, starts = pl.pallas_call(
        first_kernel,
        out_shape=(
            jax.ShapeDtypeStruct((span, 2 * head_dim), jnp.float32),
            jax.ShapeDtypeStruct((span, head_dim), jnp.float32),
            jax.ShapeDtypeStruct((span, head_dim), jnp.int32),
        ),
        in_specs=[SMEM, VMEM, HBM, VMEM],
        out_specs=(VMEM, VMEM, VMEM),
        scratch_shapes=[pltpu.VMEM((1, span), jnp.int32), both, both, pltpu.SemaphoreType.DMA],
        compiler_params=params,
        cost_estimate=cost(2),
    )(pos, queries, doc_start.reshape(1, span), held)
    return pl.pallas_call(
        second_kernel,
        out_shape=(
            jax.ShapeDtypeStruct((span, head_dim), jnp.bfloat16),
            jax.ShapeDtypeStruct((1, span), jnp.float32),
        ),
        in_specs=[SMEM, VMEM, VMEM, VMEM, VMEM, VMEM, VMEM],
        out_specs=(HBM, HBM),
        scratch_shapes=[
            both,
            both,
            both,
            pltpu.VMEM((span, head_dim), jnp.bfloat16),
            pltpu.VMEM((1, span), jnp.float32),
            pltpu.SemaphoreType.DMA((span // ROWS + 1,)),
        ],
        compiler_params=params,
        cost_estimate=cost(1),
    )(pos, queries, starts, held, other, sums, shift)


def body(queries, keys, values, doc_start):
    span, (shard, head_dim) = doc_start.shape[0], keys.shape
    count, heads = lax.axis_size("seq"), lax.axis_size("head")
    pos = lax.axis_index("seq")
    width = heads // 2
    own = jnp.where(lax.broadcasted_iota(jnp.int32, (2, shard, head_dim), 0) == 0, keys[None], values[None])
    upward = [(i, i + 4) for i in range(count - 4) if i % 4 >= 2]
    below = lax.ppermute(own, "seq", upward)
    to_side = lax.broadcasted_iota(jnp.int32, (2, 2, width) + own.shape, 1)
    sent = jnp.where((to_side == 0) & (pos % 4 >= 2), below, own)
    slabs = [
        [
            (z * 4 + side * 2 + core) * heads + high * width + (y + (side + core) * (width // 2)) % width
            for high in range(2)
            for side in range(2)
            for y in range(width)
        ]
        for z in range(count // 4)
        for core in range(2)
    ]
    held = lax.all_to_all(sent.reshape((4 * width,) + own.shape), AXES, 0, 0, axis_index_groups=slabs)
    held = held.reshape(sent.shape)
    other = lax.ppermute(held, "seq", [(i, i ^ 1) for i in range(count)])
    return attend(jnp.stack([pos]).astype(jnp.int32), queries, doc_start, held, other)


def solution(mesh):
    in_specs = (P("seq", "head"), P(("seq", "head"), None), P(("seq", "head"), None), P("seq"))
    out_specs = (P("seq", "head"), P("head", "seq"))
    return jax.shard_map(body, mesh=mesh, in_specs=in_specs, out_specs=out_specs, check_vma=False)
```
